256 devices in a mesh: dp: 32 (over y, x, core), expert: 8 (over z).
Axes of the slice: x: 4, y: 4, z: 8, core: 2. Of those that a mesh axis runs over, the one named last changes fastest.
Arguments:
- grads: bfloat16 [32, 64, 704, 1024], P('dp', 'expert'), may hold values from -1.1953125 to 1.1953125
- momentum: float32 [64, 704, 1024], P('expert', 'dp'), may hold values from -6 to 6
Outputs:
- momentum_out: float32 [64, 704, 1024], P('expert', 'dp')
- update: bfloat16 [64, 704, 1024], P('expert', 'dp')
The draws below stay inside these ranges and needn't reach their ends.
All inputs are finite; a program needn't handle non-finite values.
Results may differ from the reference program's by a relative error of at most 0.04.
Values may be sent and summed in bfloat16 or wider, within the bound.
A program may use at most 128 MiB of HBM per device.

```python
import math
import jax
import jax.numpy as jnp
from jax import lax

D = 1024
HID = 704
ITERS = 3
EXPERTS = 64
DP_GROUPS = 32


def raised(result, own_key, source, target, shards_of, factor):
    owner, partner = [(jnp.arange(result.shape[position]) // (result.shape[position] // shards_of)).reshape([-1 if axis == position else 1 for axis in range(result.ndim)]) for position in (source, target)]
    chosen = jax.random.permutation(own_key, shards_of)[partner]
    strong = (owner == chosen) | (owner == (partner + shards_of // 2) % shards_of)
    return jnp.where(strong, factor * result, result)


def level_of(stream_key, extent, shards, low, largest):
    level = 1.0
    for axis_at, shards_of in shards:
        steps = jax.random.uniform(jax.random.fold_in(jax.random.fold_in(stream_key, 6), axis_at), (shards_of,), jnp.float32, low / len(shards), largest / len(shards))
        level = level * jnp.repeat(jnp.exp(steps), extent[axis_at] // shards_of).reshape((-1,) + (1,) * (len(extent) - 1 - axis_at))
    return level


def bell_draw(stream_key, extent, width, most, split=(), kind=jnp.bfloat16):
    gain = level_of(stream_key, extent, split, -0.22, 0.18) if split else 1.0
    entries = jax.random.normal(stream_key, extent, jnp.float32) * width * gain
    return jnp.minimum(jnp.maximum(entries, -most), most).astype(kind)


def noise_with(rng, shape, width, most, pieces, heavy, held_as=jnp.bfloat16):
    result = width * jax.random.normal(rng, shape, jnp.float32)
    if pieces:
        result = result * level_of(rng, shape, pieces, -0.22, 0.18)
    return jnp.clip(raised(result, jax.random.fold_in(rng, 3), *heavy), -most, most).astype(held_as)


def setup_inputs(seed: int = 0) -> dict:
    keys = jax.random.split(jax.random.key(seed), 3)
    return {
        "grads": noise_with(keys[0], (DP_GROUPS, EXPERTS, HID, D), 0.2, 1.1953125, ((0, 32), (1, 8)), (0, 2, 32, 2.75)),
        "momentum": bell_draw(keys[1], (EXPERTS, HID, D), 1.0, 6.0, ((0, 8), (1, 32)), jnp.float32),
    }


coef_a = 3.4445
coef_b = -4.775
coef_c = 2.0315
beta_momentum = 0.95
norm_eps = 1e-07

def contract_rows(left, right):
    return lax.dot_general(left, right, (((1,), (1,)), ((), ())), preferred_element_type=jnp.float32)

def newton_schulz(matrix):
    rows_count, cols_count = matrix.shape
    values = matrix.astype(jnp.float32)
    total = jnp.sum(values * values)
    iterate = (values / (jnp.sqrt(total) + norm_eps)).astype(jnp.bfloat16)
    for turn in range(ITERS):
        gram_matrix = contract_rows(iterate, iterate).astype(jnp.bfloat16)
        squared = jnp.dot(gram_matrix, gram_matrix, preferred_element_type=jnp.float32)
        polynomial = (coef_b * gram_matrix.astype(jnp.float32) + coef_c * squared).astype(jnp.bfloat16)
        mixed = jnp.dot(polynomial, iterate, preferred_element_type=jnp.float32)
        iterate = (coef_a * iterate.astype(jnp.float32) + mixed).astype(jnp.bfloat16)
    factor = math.sqrt(max(rows_count, cols_count))
    return (iterate.astype(jnp.float32) * factor).astype(jnp.bfloat16)

def reference(grads, momentum):

    def one_expert(expert):
        local_grads = lax.dynamic_index_in_dim(grads, expert, 1, keepdims=False)
        grad_sum = lax.optimization_barrier(jnp.sum(local_grads.astype(jnp.float32), axis=0))
        previous = lax.dynamic_index_in_dim(momentum, expert, 0, keepdims=False)
        momentum_new = beta_momentum * previous + grad_sum
        blended = (grad_sum + beta_momentum * momentum_new).astype(jnp.bfloat16)
        return (momentum_new, newton_schulz(blended))
    momentum_out, update = lax.map(one_expert, jnp.arange(EXPERTS, dtype=jnp.int32))
    return (momentum_out, update)
```

```python
import functools

import jax
import jax.numpy as jnp
from jax import lax
from jax.experimental import pallas as pl
from jax.experimental.pallas import tpu as pltpu
from jax.sharding import PartitionSpec as P

MESH = pl.DeviceIdType.MESH
ITERS = 3
A, B, C = 3.4445, -4.775, 2.0315
BETA = 0.95
EPS = 1e-07

SIDE = 4
CHIPS = SIDE * SIDE
EXPERTS = 8
MINE = 4
HID, D = 704, 1024
ROWS = HID // CHIPS
SLOT = 48
HELD = 720
OWN = HID // (2 * CHIPS)
ROUNDS = 4
W = D // ROUNDS
TALL = CHIPS * SLOT
LANES = 128
STEP = 192


def kernel(grads, mom, mo_out, up_out, own, got, stage, r1, r2, p2, r3, bl, mm, mo,
           xa, xb, gb, up, own_s, die_ss, die_rs, s1_s, s1_r, s2_s, s2_r, h_s, h_r,
           p_s, p_r, g_s, g_r, m_l, m_s, m_r, mo_l, mo_s, mo_r, u_s, u_r):
    me = lax.axis_index("dp")
    z = lax.axis_index("expert")
    c = me % 2
    x = (me // 2) % SIDE
    y = me // (2 * SIDE)
    a = jnp.where(c == 0, x, y)
    b = jnp.where(c == 0, y, x)

    def at(a_, b_):
        a_, b_ = a_ % SIDE, b_ % SIDE
        row = jnp.where(c == 0, b_, a_)
        col = jnp.where(c == 0, a_, b_)
        return ((row * SIDE + col) * 2 + c, z)

    sib = (me + 1 - 2 * c, z)
    an, ap = at(a + 1, b), at(a + 3, b)
    bn, bp, bo = at(a, b + 1), at(a, b + 3), at(a, b + 2)
    a1, a2, a3 = (a + 1) % SIDE, (a + 2) % SIDE, (a + 3) % SIDE
    b1, b2, b3 = (b + 1) % SIDE, (b + 2) % SIDE, (b + 3) % SIDE

    def remote(src, dst, ss, rs, dev):
        return pltpu.make_async_remote_copy(
            src, dst, ss, rs, device_id=dev, device_id_type=MESH)

    barrier = pltpu.get_barrier_semaphore()
    for dev in (sib, an, ap, bn, bp, bo):
        pl.semaphore_signal(barrier, inc=1, device_id=dev, device_id_type=MESH)
    pl.semaphore_wait(barrier, 6)

    def cols(q):
        return pl.ds(q * W, W)

    def die(q):
        return remote(
            grads.at[pl.ds(MINE * (1 - c), MINE), :, cols(q)],
            got.at[q, :, pl.ds(0, HID), :], die_ss.at[q], die_rs.at[q], sib)

    def load(q):
        return pltpu.make_async_copy(
            grads.at[pl.ds(MINE * c, MINE), :, cols(q)],
            own.at[q, :, pl.ds(0, HID), :], own_s.at[q])

    die(0).start()
    load(0).start()
    die(1).start()
    load(1).start()
    held = pl.ds(pl.multiple_of(OWN * EXPERTS * c, 8), OWN * EXPERTS)
    my_m = [pltpu.make_async_copy(
        mom.at[:, pl.ds(LANES * n, LANES)], mm.at[n, held], m_l.at[n]) for n in range(D // LANES)]
    his_m = [remote(mom.at[:, pl.ds(LANES * n, LANES)], mm.at[n, held], m_s.at[n], m_r.at[n], sib)
             for n in range(D // LANES)]
    for cp in my_m + his_m:
        cp.start()

    half = SIDE // 2

    def first(q):
        up_half = remote(stage.at[q, a2, pl.ds(0, half)], r1.at[q, 0],
                         s1_s.at[q, 0], s1_r.at[q, 0], an)
        down_half = remote(stage.at[q, a2, pl.ds(half, half)], r1.at[q, 1],
                           s1_s.at[q, 1], s1_r.at[q, 1], ap)
        return up_half, down_half

    def alone(q):
        to_next = remote(stage.at[q, a1, pl.ds(half, half)], r2.at[q, 0, pl.ds(half, half)],
                         h_s.at[q, 0], h_r.at[q, 0], an)
        to_prev = remote(stage.at[q, a3, pl.ds(0, half)], r2.at[q, 1, pl.ds(0, half)],
                         h_s.at[q, 1], h_r.at[q, 1], ap)
        return to_next, to_prev

    def second(q):
        to_next = remote(stage.at[q, a1, pl.ds(0, half)], r2.at[q, 0, pl.ds(0, half)],
                         s2_s.at[q, 0], s2_r.at[q, 0], an)
        to_prev = remote(stage.at[q, a3, pl.ds(half, half)], r2.at[q, 1, pl.ds(half, half)],
                         s2_s.at[q, 1], s2_r.at[q, 1], ap)
        return to_next, to_prev

    def third(q):
        return [remote(p2.at[q, t], r3.at[q, i], p_s.at[q, i], p_r.at[q, i], dev)
                for i, (t, dev) in enumerate(((b1, bn), (b3, bp), (b2, bo)))]

    def do_die(q):
        if q + 2 < ROUNDS:
            die(q + 2).start()
            load(q + 2).start()
        load(q).wait()
        die(q).wait_recv()

        def one(e, _):
            for k in range(CHIPS):
                ky, kx = k // SIDE, k % SIDE
                ka = jnp.where(c == 0, kx, ky)
                kb = jnp.where(c == 0, ky, kx)
                rows = pl.ds(ROWS * k, SLOT)
                stage[q, ka, kb, e] = own[q, e, rows, :] + got[q, e, rows, :]
            return 0

        lax.fori_loop(0, MINE, one, 0)
        for cp in first(q) + alone(q):
            cp.start()

    def do_mid(q):
        for side, (tgt, lo) in enumerate(((a1, 0), (a3, half))):
            first(q)[side].wait_recv()

            def one(e, _):
                for k in range(half):
                    stage[q, tgt, lo + k, e] = stage[q, tgt, lo + k, e] + r1[q, side, k, e]
                return 0

            lax.fori_loop(0, MINE, one, 0)
            second(q)[side].start()

    def do_sum(q):
        for cp in alone(q) + second(q):
            cp.wait_recv()

        def one(e, _):
            for k in range(SIDE):
                total = stage[q, a, k, e].astype(jnp.float32) + r2[q, 0, k, e].astype(jnp.float32)
                p2[q, k, e] = (total + r2[q, 1, k, e].astype(jnp.float32)).astype(jnp.bfloat16)
            return 0

        lax.fori_loop(0, MINE, one, 0)
        for cp in third(q):
            cp.start()

    def owner(e):
        oy = e // 2
        ox = oy % 2 + 2 * (e % 2)
        return ((oy * SIDE + ox) * 2 + e // MINE)

    chip = me // 2

    def gather(q, j):
        return remote(bl.at[q, j], xa.at[pl.ds(SLOT * chip, SLOT), cols(q)], g_s.at[q, j],
                      g_r.at[q], (owner(MINE * c + j), z))

    def gather_own(q, j):
        return pltpu.make_async_copy(
            bl.at[q, j], xa.at[pl.ds(SLOT * chip, SLOT), cols(q)], g_r.at[q])

    real = lax.broadcasted_iota(jnp.int32, (SLOT, W), 0) < ROWS

    def do_blend(q):
        for cp in third(q):
            cp.wait_recv()
        if q == 0:
            for cp in my_m + his_m:
                cp.wait()

        def one(j, _):
            total = p2[q, b, j].astype(jnp.float32)
            for i in range(3):
                total = total + r3[q, i, j].astype(jnp.float32)
            before = jnp.concatenate(
                [mm[n, pl.ds(MINE * c + j, SLOT, stride=EXPERTS), :]
                 for n in range(q * W // LANES, (q + 1) * W // LANES)], axis=1)
            after = BETA * before + total
            mo[j, :, cols(q)] = after
            bl[q, j] = jnp.where(real, total + BETA * after, 0.0).astype(jnp.bfloat16)
            there = owner(MINE * c + j)

            @pl.when(there != me)
            def _():
                gather(q, j).start()

            @pl.when(there == me)
            def _():
                gather_own(q, j).start()

            return 0

        lax.fori_loop(0, MINE, one, 0)

    for t in range(ROUNDS + 3):
        if t < ROUNDS:
            do_die(t)
        if 0 <= t - 1 < ROUNDS:
            do_mid(t - 1)
        if 0 <= t - 2 < ROUNDS:
            do_sum(t - 2)
        if 0 <= t - 3 < ROUNDS:
            do_blend(t - 3)

    def window(core):
        return pl.ds(pl.multiple_of(16 * core, 16), 32)

    my_mo = pltpu.make_async_copy(
        mo.at[:, window(c), :], mo_out.at[pl.ds(MINE * c, MINE)], mo_l)
    his_mo = remote(
        mo.at[:, window(1 - c), :], mo_out.at[pl.ds(MINE * c, MINE)], mo_s, mo_r, sib)
    my_mo.start()
    his_mo.start()

    mine = 2 * y + x // 2

    def give(dev):
        k, core = dev // 2, dev % 2
        rows = pl.ds(pl.multiple_of(SLOT * k + 16 * core, 16), 32)
        return remote(up.at[rows, :], up_out.at[mine], u_s.at[dev], u_r, (dev, z))

    def give_own():
        rows = pl.ds(pl.multiple_of(SLOT * chip + 16 * c, 16), 32)
        return pltpu.make_async_copy(up.at[rows, :], up_out.at[mine], u_r)

    @pl.when((x % 2 == y % 2) & (c == y // 2))
    def _():
        for q in range(ROUNDS):
            pltpu.make_async_copy(xa.at[:, cols(q)], xa.at[:, cols(q)], g_r.at[q]).wait()
        steps = TALL // STEP

        def span(i):
            return pl.ds(pl.multiple_of(i * STEP, STEP), STEP)

        def squares(i, acc):
            v = xa[span(i), :].astype(jnp.float32)
            return acc + jnp.sum(v * v, axis=0, keepdims=True)

        total = jnp.sum(lax.fori_loop(0, steps, squares, jnp.zeros((1, D), jnp.float32)),
                        axis=1, keepdims=True)
        scale = 1.0 / (jnp.sqrt(total) + EPS)

        def normalise(i, _):
            xa[span(i), :] = (xa[span(i), :].astype(jnp.float32) * scale).astype(jnp.bfloat16)
            return 0

        lax.fori_loop(0, steps, normalise, 0)

        src, dst = xa, xb
        for turn in range(ITERS):
            last = turn == ITERS - 1

            def gram(i, _, src=src):
                gb[span(i), :] = lax.dot_general(
                    src[span(i), :], src[...], (((1,), (1,)), ((), ())),
                    preferred_element_type=jnp.float32).astype(jnp.bfloat16)
                return 0

            lax.fori_loop(0, steps, gram, 0)

            def apply(i, _, src=src, dst=dst, last=last):
                g = gb[span(i), :]
                squared = jnp.dot(g, gb[...], preferred_element_type=jnp.float32)
                poly = (B * g.astype(jnp.float32) + C * squared).astype(jnp.bfloat16)
                mixed = jnp.dot(poly, src[...], preferred_element_type=jnp.float32)
                new = (A * src[span(i), :].astype(jnp.float32) + mixed)
                if not last:
                    dst[span(i), :] = new.astype(jnp.bfloat16)
                    return 0
                up[span(i), :] = (new.astype(jnp.bfloat16) * 32.0).astype(jnp.bfloat16)

                def send(n, _):
                    dev = i * 2 * (STEP // SLOT) + n

                    @pl.when(dev != me)
                    def _():
                        give(dev).start()

                    @pl.when(dev == me)
                    def _():
                        give_own().start()

                    return 0

                lax.fori_loop(0, 2 * (STEP // SLOT), send, 0)
                return 0

            lax.fori_loop(0, steps, apply, 0)
            src, dst = dst, src

        def sent(dev, _):
            @pl.when(dev != me)
            def _():
                give(dev).wait_send()
            return 0

        lax.fori_loop(0, 2 * CHIPS, sent, 0)

    for q in range(ROUNDS):
        die(q).wait_send()
        for cp in first(q) + alone(q) + second(q):
            cp.wait_send()
        for cp in third(q):
            cp.wait_send()

        def sent(j, _, q=q):
            @pl.when(owner(MINE * c + j) != me)
            def _():
                gather(q, j).wait_send()
            return 0

        lax.fori_loop(0, MINE, sent, 0)
    my_mo.wait()
    his_mo.wait()
    pltpu.make_async_copy(up_out, up_out, u_r).wait()


def reduce_and_step(grads, mom):
    bf, f32 = jnp.bfloat16, jnp.float32
    dma = pltpu.SemaphoreType.DMA
    half = SIDE // 2
    return pl.pallas_call(
        kernel,
        out_shape=(
            jax.ShapeDtypeStruct((EXPERTS, 32, D), f32),
            jax.ShapeDtypeStruct((EXPERTS, 32, D), bf),
        ),
        in_specs=[pl.BlockSpec(memory_space=pl.ANY)] * 2,
        out_specs=(pl.BlockSpec(memory_space=pl.ANY),) * 2,
        scratch_shapes=[
            pltpu.VMEM((ROUNDS, MINE, HELD, W), bf),
            pltpu.VMEM((ROUNDS, MINE, HELD, W), bf),
            pltpu.VMEM((ROUNDS, SIDE, SIDE, MINE, SLOT, W), bf),
            pltpu.VMEM((ROUNDS, 2, half, MINE, SLOT, W), bf),
            pltpu.VMEM((ROUNDS, 2, SIDE, MINE, SLOT, W), bf),
            pltpu.VMEM((ROUNDS, SIDE, MINE, SLOT, W), bf),
            pltpu.VMEM((ROUNDS, 3, MINE, SLOT, W), bf),
            pltpu.VMEM((ROUNDS, MINE, SLOT, W), bf),
            pltpu.VMEM((D // LANES, SLOT * EXPERTS, LANES), f32),
            pltpu.VMEM((MINE, SLOT, D), f32),
            pltpu.VMEM((TALL, D), bf),
            pltpu.VMEM((TALL, D), bf),
            pltpu.VMEM((TALL, TALL), bf),
            pltpu.VMEM((TALL, D), bf),
            dma((ROUNDS,)), dma((ROUNDS,)), dma((ROUNDS,)),
            dma((ROUNDS, 2)), dma((ROUNDS, 2)),
            dma((ROUNDS, 2)), dma((ROUNDS, 2)),
            dma((ROUNDS, 2)), dma((ROUNDS, 2)),
            dma((ROUNDS, 3)), dma((ROUNDS, 3)),
            dma((ROUNDS, MINE)), dma((ROUNDS,)),
            dma((D // LANES,)), dma((D // LANES,)), dma((D // LANES,)),
            dma(()), dma(()), dma(()),
            dma((2 * CHIPS,)), dma(()),
        ],
        compiler_params=pltpu.CompilerParams(
            collective_id=0, has_side_effects=True, vmem_limit_bytes=60 * 2**20),
        name="muon",
    )(grads, mom)


def per_device(grads, momentum):
    c = lax.axis_index("dp") % 2
    mom = jnp.transpose(momentum, (1, 0, 2)).reshape(OWN * EXPERTS, D)
    mo, up = reduce_and_step(grads[0], mom)
    skip = (OWN - 16) * c
    return (lax.dynamic_slice_in_dim(mo, skip, OWN, 1), lax.dynamic_slice_in_dim(up, skip, OWN, 1))


def solution(mesh):
    return jax.shard_map(
        per_device,
        mesh=mesh,
        in_specs=(P("dp", "expert", None, None), P("expert", "dp", None)),
        out_specs=(P("expert", "dp", None), P("expert", "dp", None)),
        check_vma=False,
    )
```

```python
import functools

import jax
import jax.numpy as jnp
from jax import lax
from jax.experimental import pallas as pl
from jax.experimental.pallas import tpu as pltpu
from jax.sharding import PartitionSpec as P

MESH = pl.DeviceIdType.MESH
ITERS = 3
A, B, C = 3.4445, -4.775, 2.0315
BETA = 0.95
EPS = 1e-07

SIDE = 4
CHIPS = SIDE * SIDE
EXPERTS = 8
MINE = 4
HID, D = 704, 1024
ROWS = HID // CHIPS
SLOT = 48
QUARTER = HID // SIDE
OWN = HID // (2 * CHIPS)
ROUNDS = 8
DIRECT = 3
RELAYED = 5
W = D // ROUNDS
TALL = CHIPS * SLOT
LANES = 128
LEFT = 512
PARTS = 2
PART = LEFT // PARTS
BLOCK = 256
STRIP = 128


def kernel(grads, mom, mo_out, up_out, own, got, stage, r1a, r2a, p2, r1b, r2b, r3, bl, mm, ms,
           xa, xb, gb, pb, up, rb, lb, own_s, die_ss, die_rs, s1_s, s1_r, s2_s, s2_r, h_s, h_r,
           p_s, p_r, g_s, g_r, b_s, b_r, m_l, m_s, m_r, mo_l, mo_s, mo_r, l_s, l_r, v_s, u_s, u_r):
    me = lax.axis_index("dp")
    z = lax.axis_index("expert")
    c = me % 2
    x = (me // 2) % SIDE
    y = me // (2 * SIDE)
    a = jnp.where(c == 0, x, y)
    b = jnp.where(c == 0, y, x)

    def at(a_, b_):
        a_, b_ = a_ % SIDE, b_ % SIDE
        row = jnp.where(c == 0, b_, a_)
        col = jnp.where(c == 0, a_, b_)
        return ((row * SIDE + col) * 2 + c, z)

    sib = (me + 1 - 2 * c, z)
    an, ap = at(a + 1, b), at(a + 3, b)
    bn, bp, bo = at(a, b + 1), at(a, b + 3), at(a, b + 2)
    a1, a2, a3 = (a + 1) % SIDE, (a + 2) % SIDE, (a + 3) % SIDE
    b1, b2, b3 = (b + 1) % SIDE, (b + 2) % SIDE, (b + 3) % SIDE

    def remote(src, dst, ss, rs, dev):
        return pltpu.make_async_remote_copy(
            src, dst, ss, rs, device_id=dev, device_id_type=MESH)

    def cols(q):
        return pl.ds(q * W, W)

    def load(q):
        return pltpu.make_async_copy(
            grads.at[pl.ds(MINE * c, MINE), :, cols(q)], own.at[q], own_s.at[q])

    load(0).start()
    load(1).start()

    barrier = pltpu.get_barrier_semaphore()
    for dev in (sib, an, ap, bn, bp, bo):
        pl.semaphore_signal(barrier, inc=1, device_id=dev, device_id_type=MESH)
    pl.semaphore_wait(barrier, 6)

    def die(q):
        return remote(grads.at[pl.ds(MINE * (1 - c), MINE), :, cols(q)], got.at[q],
                      die_ss.at[q], die_rs.at[q], sib)

    die(0).start()
    die(1).start()
    held = pl.ds(pl.multiple_of(OWN * EXPERTS * c, 8), OWN * EXPERTS)
    my_m = [pltpu.make_async_copy(
        mom.at[:, pl.ds(LANES * n, LANES)], mm.at[n, held], m_l.at[n]) for n in range(D // LANES)]
    his_m = [remote(mom.at[:, pl.ds(LANES * n, LANES)], mm.at[n, held], m_s.at[n], m_r.at[n], sib)
             for n in range(D // LANES)]
    for cp in my_m + his_m:
        cp.start()

    half = MINE // 2
    lower, upper = pl.ds(0, half), pl.ds(half, half)

    ringed = ROUNDS - DIRECT
    phases = ((stage, r1a, r2a, (a1, a2, a3), an, ap), (p2, r1b, r2b, (b1, b2, b3), bn, bp))

    def first(f, q):
        src, r1, _, (_, far, _), following, previous = phases[f]
        return (remote(src.at[q, far, lower], r1.at[q, 0], s1_s.at[f, q, 0], s1_r.at[f, q, 0],
                       following),
                remote(src.at[q, far, upper], r1.at[q, 1], s1_s.at[f, q, 1], s1_r.at[f, q, 1],
                       previous))

    def alone(f, q):
        src, _, r2, (near, _, back), following, previous = phases[f]
        return (remote(src.at[q, near, upper], r2.at[q, 0, upper], h_s.at[f, q, 0],
                       h_r.at[f, q, 0], following),
                remote(src.at[q, back, lower], r2.at[q, 1, lower], h_s.at[f, q, 1],
                       h_r.at[f, q, 1], previous))

    def second(f, q):
        src, _, r2, (near, _, back), following, previous = phases[f]
        return (remote(src.at[q, near, lower], r2.at[q, 0, lower], s2_s.at[f, q, 0],
                       s2_r.at[f, q, 0], following),
                remote(src.at[q, back, upper], r2.at[q, 1, upper], s2_s.at[f, q, 1],
                       s2_r.at[f, q, 1], previous))

    def third(q):
        d = q - ringed
        return [remote(p2.at[q, t], r3.at[d, i], p_s.at[d, i], p_r.at[d, i], dev)
                for i, (t, dev) in enumerate(((b1, bn), (b3, bp), (b2, bo)))]

    def do_die(q):
        if q + 2 < ROUNDS:
            die(q + 2).start()
            load(q + 2).start()
        load(q).wait()
        die(q).wait_recv()

        @pl.when(c == 1)
        def _():
            def one(e, _):
                for k in range(SIDE):
                    rows = pl.ds(QUARTER * k, QUARTER)
                    stage[q, k, e] = own[q, e, rows, :] + got[q, e, rows, :]
                return 0

            lax.fori_loop(0, MINE, one, 0)

        @pl.when(c == 0)
        def _():
            def one(e, _):
                for k in range(CHIPS):
                    rows = pl.ds(ROWS * k, ROWS)
                    stage[q, k % SIDE, e, pl.ds(ROWS * (k // SIDE), ROWS), :] = (
                        own[q, e, rows, :] + got[q, e, rows, :])
                return 0

            lax.fori_loop(0, MINE, one, 0)

        for cp in first(0, q) + alone(0, q):
            cp.start()

    def do_mid(f, q):
        src, r1, _, (near, _, back), _, _ = phases[f]
        for side, (tgt, lo) in enumerate(((near, 0), (back, half))):
            first(f, q)[side].wait_recv()

            def one(e, _):
                src[q, tgt, lo + e] = src[q, tgt, lo + e] + r1[q, side, e]
                return 0

            lax.fori_loop(0, half, one, 0)
            second(f, q)[side].start()

    def do_sum(q):
        for cp in alone(0, q) + second(0, q):
            cp.wait_recv()

        def one(e, _):
            total = stage[q, a, e].astype(jnp.float32) + r2a[q, 0, e].astype(jnp.float32)
            total = total + r2a[q, 1, e].astype(jnp.float32)
            for k in range(SIDE):
                p2[q, k, e, pl.ds(0, ROWS), :] = (
                    total[ROWS * k:ROWS * (k + 1)].astype(jnp.bfloat16))
            return 0

        lax.fori_loop(0, MINE, one, 0)
        for cp in third(q) if q >= ringed else first(1, q) + alone(1, q):
            cp.start()

    def owner(e):
        oy = e // 2
        ox = oy % 2 + 2 * (e % 2)
        return oy, ox, (oy * SIDE + ox) * 2 + e // MINE

    chip = me // 2
    here = pl.ds(pl.multiple_of(SLOT * chip, 16), SLOT)

    def gather(q, j, dev):
        return remote(bl.at[q, j], xa.at[here, cols(q)], g_s.at[q, j], g_r.at[q], (dev, z))

    def gather_own(q, j):
        return pltpu.make_async_copy(bl.at[q, j], xa.at[here, cols(q)], g_r.at[q])

    def gather_row(q, j, oy):
        row = (y - oy) % SIDE - 1
        return remote(bl.at[q, j], rb.at[q, row], g_s.at[q, j], b_r.at[q, row],
                      ((oy * SIDE + x) * 2 + c, z))

    def relay(q, row):
        there = pl.ds(pl.multiple_of(SLOT * (((y + row + 1) % SIDE) * SIDE + x), 16), SLOT)
        dev = (y * SIDE + y % 2 + 2 * (q % 2)) * 2 + c
        return remote(rb.at[q, row], xa.at[there, cols(q)], b_s.at[q, row], g_r.at[q], (dev, z))

    def relays(q):
        return (c == y // 2) & (x != y % 2 + 2 * (q % 2))

    def do_relay(q):
        @pl.when(relays(q))
        def _():
            for row in range(SIDE - 1):
                landed = rb.at[q, row]
                pltpu.make_async_copy(landed, landed, b_r.at[q, row]).wait()
                relay(q, row).start()

    real = lax.broadcasted_iota(jnp.int32, (SLOT, W), 0) < ROWS

    def do_blend(q):
        for cp in third(q) if q >= ringed else alone(1, q) + second(1, q):
            cp.wait_recv()
        came = ([r3.at[q - ringed, i] for i in range(3)] if q >= ringed
                else [r2b.at[q, i] for i in range(2)])
        if q == 0:
            for cp in my_m + his_m:
                cp.wait()

        def one(j, _):
            total = p2[q, b, j].astype(jnp.float32)
            for ref in came:
                total = total + ref[j].astype(jnp.float32)
            turns = range(q * W // LANES, (q + 1) * W // LANES)
            these = pl.ds(MINE * c + j, SLOT, stride=EXPERTS)
            before = jnp.concatenate([mm[n, these, :] for n in turns], axis=1)
            after = BETA * before + total
            for i, n in enumerate(turns):
                mm[n, these, :] = after[:, i * LANES:(i + 1) * LANES]
            bl[q, j] = jnp.where(real, total + BETA * after, 0.0).astype(jnp.bfloat16)
            oy, ox, there = owner(MINE * c + j)
            turned = (x != ox) & (y != oy) & (j % 2 == q % 2) if q < RELAYED else False

            @pl.when(there == me)
            def _():
                gather_own(q, j).start()

            @pl.when((there != me) & jnp.logical_not(turned))
            def _():
                gather(q, j, there).start()

            if q < RELAYED:
                @pl.when(turned)
                def _():
                    gather_row(q, j, oy).start()

            return 0

        lax.fori_loop(0, MINE, one, 0)

    for t in range(ROUNDS + 4):
        if t < ROUNDS:
            do_die(t)
        if 0 <= t - 1 < ROUNDS:
            do_mid(0, t - 1)
        if 0 <= t - 2 < ROUNDS:
            do_sum(t - 2)
        if 0 <= t - 3 < ringed:
            do_mid(1, t - 3)
        if 0 <= t - 4 < ringed:
            do_blend(t - 4)
        if 0 <= t - 5 < RELAYED:
            do_relay(t - 5)
        if ringed <= t - 3 < ROUNDS:
            do_blend(t - 3)

    def share(core):
        return pl.ds(pl.multiple_of(OWN * EXPERTS * core, 8), OWN * EXPERTS)

    my_mo = [pltpu.make_async_copy(
        mm.at[n, share(c)], mo_out.at[:, pl.ds(LANES * n, LANES)], mo_l.at[n])
        for n in range(D // LANES)]
    his_mo = [remote(mm.at[n, share(1 - c)], ms.at[n], mo_s.at[n], mo_r.at[n], sib)
              for n in range(D // LANES)]
    for cp in his_mo:
        cp.start()

    def finish_mo():
        row = lax.broadcasted_iota(jnp.int32, (OWN * EXPERTS, LANES), 0)
        ours = (row % EXPERTS) // MINE == c
        for n in range(D // LANES):
            his_mo[n].wait_recv()
            mm[n, share(c), :] = jnp.where(ours, mm[n, share(c), :], ms[n])
            my_mo[n].start()

    oy = x % 2 + 2 * c
    mine = 2 * oy + x // 2
    right = pl.ds(LEFT, D - LEFT)

    def left(part):
        return pl.ds(PART * part, PART)

    def give_row(part, d):
        row = (oy + d) % SIDE
        rows = pl.ds(pl.multiple_of(SIDE * SLOT * row, 16), SIDE * SLOT)
        return remote(up.at[rows, left(part)], lb.at[part], l_s.at[part, d - 1], l_r.at[part],
                      ((row * SIDE + x) * 2 + c, z))

    def give(dev):
        rows = pl.ds(pl.multiple_of(SLOT * (dev // 2) + 16 * (dev % 2), 16), 32)
        return remote(up.at[rows, right], up_out.at[mine, :, right], u_s.at[dev], u_r, (dev, z))

    def give_own():
        rows = pl.ds(pl.multiple_of(SLOT * chip + 16 * c, 16), 32)
        return pltpu.make_async_copy(up.at[rows, right], up_out.at[mine, :, right], u_r)

    def spread(src, base, part, n):
        dev = (y * SIDE) * 2 + n
        rows = pl.ds(pl.multiple_of(base + SLOT * (n // 2) + 16 * (n % 2), 16), 32)
        return remote(src.at[rows], up_out.at[mine, :, left(part)], v_s.at[part, n], u_r, (dev, z))

    def spread_all(src, base, part):
        def one(n, _):
            @pl.when(y * SIDE * 2 + n != me)
            def _():
                spread(src, base, part, n).start()
            return 0

        lax.fori_loop(0, 2 * SIDE, one, 0)
        rows = pl.ds(pl.multiple_of(base + SLOT * x + 16 * c, 16), 32)
        pltpu.make_async_copy(src.at[rows], up_out.at[mine, :, left(part)], u_r).start()

    @pl.when(y == oy)
    def _():
        for q in range(ROUNDS):
            pltpu.make_async_copy(xa.at[:, cols(q)], xa.at[:, cols(q)], g_r.at[q]).wait()
        blocks = [slice(i * BLOCK, (i + 1) * BLOCK) for i in range(TALL // BLOCK)]
        strips = [slice(i * STRIP, (i + 1) * STRIP) for i in range(TALL // STRIP)]
        total = jnp.zeros((1, D), jnp.float32)
        for rows in strips:
            v = xa[rows, :].astype(jnp.float32)
            total = total + jnp.sum(v * v, axis=0, keepdims=True)
        scale = 1.0 / (jnp.sqrt(jnp.sum(total, axis=1, keepdims=True)) + EPS)
        for rows in strips:
            xa[rows, :] = (xa[rows, :].astype(jnp.float32) * scale).astype(jnp.bfloat16)

        src, dst = xa, xb
        for turn in range(ITERS):
            for i, rows in enumerate(blocks):
                for j in range(i, len(blocks)):
                    block = lax.dot_general(
                        src[rows, :], src[blocks[j], :], (((1,), (1,)), ((), ())),
                        preferred_element_type=jnp.float32)
                    gb[rows, blocks[j]] = block.astype(jnp.bfloat16)
                    if j > i:
                        gb[blocks[j], rows] = block.T.astype(jnp.bfloat16)
            for i, rows in enumerate(blocks):
                for j in range(i, len(blocks)):
                    squared = jnp.dot(gb[rows, :], gb[:, blocks[j]],
                                      preferred_element_type=jnp.float32)
                    poly = (B * gb[rows, blocks[j]].astype(jnp.float32)
                            + C * squared).astype(jnp.bfloat16)
                    pb[rows, blocks[j]] = poly
                    if j > i:
                        pb[blocks[j], rows] = poly.T
            if turn < ITERS - 1:
                for rows in strips:
                    mixed = jnp.dot(pb[rows, :], src[...], preferred_element_type=jnp.float32)
                    dst[rows, :] = (A * src[rows, :].astype(jnp.float32) + mixed).astype(
                        jnp.bfloat16)
                src, dst = dst, src
                continue
            for part in range(PARTS + 1):
                these = slice(PART * part, PART * (part + 1) if part < PARTS else D)
                for rows in strips:
                    mixed = jnp.dot(pb[rows, :], src[:, these], preferred_element_type=jnp.float32)
                    new = (A * src[rows, these].astype(jnp.float32) + mixed).astype(jnp.bfloat16)
                    up[rows, these] = (new.astype(jnp.float32) * 32.0).astype(jnp.bfloat16)
                if part < PARTS:
                    for d in (2, 1, 3):
                        give_row(part, d).start()
                    spread_all(up.at[:, left(part)], SIDE * SLOT * y, part)

        def send(dev, _):
            @pl.when(dev != me)
            def _():
                give(dev).start()
            return 0

        lax.fori_loop(0, 2 * CHIPS, send, 0)
        give_own().start()
        finish_mo()

        def sent(dev, _):
            @pl.when(dev != me)
            def _():
                give(dev).wait_send()
            return 0

        lax.fori_loop(0, 2 * CHIPS, sent, 0)
        for part in range(PARTS):
            for d in range(1, SIDE):
                give_row(part, d).wait_send()

    @pl.when(y != oy)
    def _():
        finish_mo()
        for part in range(PARTS):
            give_row(part, 1).wait_recv()
            spread_all(lb.at[part], 0, part)

    for q in range(ROUNDS):
        die(q).wait_send()
        for f in range(2):
            if f == 0 or q < ringed:
                for cp in first(f, q) + alone(f, q) + second(f, q):
                    cp.wait_send()
        if q >= ringed:
            for cp in third(q):
                cp.wait_send()

        def sent(j, _, q=q):
            @pl.when(owner(MINE * c + j)[2] != me)
            def _():
                gather(q, j, sib[0]).wait_send()
            return 0

        lax.fori_loop(0, MINE, sent, 0)
        if q < RELAYED:
            @pl.when(relays(q))
            def _(q=q):
                for row in range(SIDE - 1):
                    relay(q, row).wait_send()
    for n in range(D // LANES):
        his_mo[n].wait_send()
        my_mo[n].wait()

    for part in range(PARTS):
        def spread_sent(n, _, part=part):
            @pl.when(y * SIDE * 2 + n != me)
            def _():
                spread(lb.at[part], 0, part, n).wait_send()
            return 0

        lax.fori_loop(0, 2 * SIDE, spread_sent, 0)
    pltpu.make_async_copy(up_out, up_out, u_r).wait()


def reduce_and_step(grads, mom):
    bf, f32 = jnp.bfloat16, jnp.float32
    dma = pltpu.SemaphoreType.DMA
    half = MINE // 2
    tiles = D // LANES
    return pl.pallas_call(
        kernel,
        out_shape=(
            jax.ShapeDtypeStruct((OWN * EXPERTS, D), f32),
            jax.ShapeDtypeStruct((EXPERTS, 32, D), bf),
        ),
        in_specs=[pl.BlockSpec(memory_space=pl.ANY)] * 2,
        out_specs=(pl.BlockSpec(memory_space=pl.ANY),) * 2,
        scratch_shapes=[
            pltpu.VMEM((ROUNDS, MINE, HID, W), bf),
            pltpu.VMEM((ROUNDS, MINE, HID, W), bf),
            pltpu.VMEM((ROUNDS, SIDE, MINE, QUARTER, W), bf),
            pltpu.VMEM((ROUNDS, 2, half, QUARTER, W), bf),
            pltpu.VMEM((ROUNDS, 2, MINE, QUARTER, W), bf),
            pltpu.VMEM((ROUNDS, SIDE, MINE, SLOT, W), bf),
            pltpu.VMEM((ROUNDS, 2, half, SLOT, W), bf),
            pltpu.VMEM((ROUNDS, 2, MINE, SLOT, W), bf),
            pltpu.VMEM((DIRECT, 3, MINE, SLOT, W), bf),
            pltpu.VMEM((ROUNDS, MINE, SLOT, W), bf),
            pltpu.VMEM((tiles, SLOT * EXPERTS, LANES), f32),
            pltpu.VMEM((tiles, OWN * EXPERTS, LANES), f32),
            pltpu.VMEM((TALL, D), bf),
            pltpu.VMEM((TALL, D), bf),
            pltpu.VMEM((TALL, TALL), bf),
            pltpu.VMEM((TALL, TALL), bf),
            pltpu.VMEM((TALL, D), bf),
            pltpu.VMEM((RELAYED, SIDE - 1, SLOT, W), bf),
            pltpu.VMEM((PARTS, SIDE * SLOT, PART), bf),
            dma((ROUNDS,)), dma((ROUNDS,)), dma((ROUNDS,)),
            dma((2, ROUNDS, 2)), dma((2, ROUNDS, 2)),
            dma((2, ROUNDS, 2)), dma((2, ROUNDS, 2)),
            dma((2, ROUNDS, 2)), dma((2, ROUNDS, 2)),
            dma((DIRECT, 3)), dma((DIRECT, 3)),
            dma((ROUNDS, MINE)), dma((ROUNDS,)),
            dma((RELAYED, SIDE - 1)), dma((RELAYED, SIDE - 1)),
            dma((tiles,)), dma((tiles,)), dma((tiles,)),
            dma((tiles,)), dma((tiles,)), dma((tiles,)),
            dma((PARTS, SIDE - 1)), dma((PARTS,)),
            dma((PARTS, 2 * SIDE)),
            dma((2 * CHIPS,)), dma(()),
        ],
        compiler_params=pltpu.CompilerParams(
            collective_id=0, has_side_effects=True, vmem_limit_bytes=48 * 2**20),
        name="muon",
    )(grads, mom)


def per_device(grads, momentum):
    c = lax.axis_index("dp") % 2
    mom = jnp.transpose(momentum, (1, 0, 2)).reshape(OWN * EXPERTS, D)
    mo, up = reduce_and_step(grads[0], mom)
    mo = jnp.transpose(mo.reshape(OWN, EXPERTS, D), (1, 0, 2))
    return mo, lax.dynamic_slice_in_dim(up, (OWN - 16) * c, OWN, 1)


def solution(mesh):
    return jax.shard_map(
        per_device,
        mesh=mesh,
        in_specs=(P("dp", "expert", None, None), P("expert", "dp", None)),
        out_specs=(P("expert", "dp", None), P("expert", "dp", None)),
        check_vma=False,
    )
```

```python
import functools

import jax
import jax.numpy as jnp
from jax import lax
from jax.experimental import pallas as pl
from jax.experimental.pallas import tpu as pltpu
from jax.sharding import PartitionSpec as P

MESH = pl.DeviceIdType.MESH
ITERS = 3
A, B, C = 3.4445, -4.775, 2.0315
BETA = 0.95
EPS = 1e-07

SIDE = 4
CHIPS = SIDE * SIDE
EXPERTS = 8
MINE = 4
HID, D = 704, 1024
ROWS = HID // CHIPS
SLOT = 48
QUARTER = HID // SIDE
OWN = HID // (2 * CHIPS)
ROUNDS = 8
LAG = 5
DIRECT = 3
RELAYED = 2
W = D // ROUNDS
TALL = CHIPS * SLOT
LANES = 128
LEFT = 512
PARTS = 2
PART = LEFT // PARTS
BLOCK = 256
STRIP = 128
EARLY = 4


def kernel(grads, mom, mo_out, up_out, own, got, stage, r1a, r2a, p2, r1b, r2b, r3, bl, mm, ms,
           xa, xb, ga, gb, pb, up, rb, lb, own_s, die_ss, die_rs, s1_s, s1_r, s2_s, s2_r, h_s, h_r,
           p_s, p_r, g_s, g_r, b_s, b_r, m_l, m_s, m_r, mo_l, mo_s, mo_r, l_s, l_r, v_s, u_s, u_r):
    me = lax.axis_index("dp")
    z = lax.axis_index("expert")
    c = me % 2
    x = (me // 2) % SIDE
    y = me // (2 * SIDE)
    a = jnp.where(c == 0, x, y)
    b = jnp.where(c == 0, y, x)

    def at(a_, b_):
        a_, b_ = a_ % SIDE, b_ % SIDE
        row = jnp.where(c == 0, b_, a_)
        col = jnp.where(c == 0, a_, b_)
        return ((row * SIDE + col) * 2 + c, z)

    sib = (me + 1 - 2 * c, z)
    an, ap = at(a + 1, b), at(a + 3, b)
    bn, bp, bo = at(a, b + 1), at(a, b + 3), at(a, b + 2)
    a1, a2, a3 = (a + 1) % SIDE, (a + 2) % SIDE, (a + 3) % SIDE
    b1, b2, b3 = (b + 1) % SIDE, (b + 2) % SIDE, (b + 3) % SIDE

    def remote(src, dst, ss, rs, dev):
        return pltpu.make_async_remote_copy(
            src, dst, ss, rs, device_id=dev, device_id_type=MESH)

    def cols(q):
        return pl.ds(q * W, W)

    def load(q):
        return pltpu.make_async_copy(
            grads.at[pl.ds(MINE * c, MINE), :, cols(q)], own.at[q], own_s.at[q])

    load(0).start()
    load(1).start()

    barrier = pltpu.get_barrier_semaphore()
    for dev in (sib, an, ap, bn, bp, bo):
        pl.semaphore_signal(barrier, inc=1, device_id=dev, device_id_type=MESH)
    pl.semaphore_wait(barrier, 6)

    def die(q):
        return remote(grads.at[pl.ds(MINE * (1 - c), MINE), :, cols(q)], got.at[q],
                      die_ss.at[q], die_rs.at[q], sib)

    die(0).start()
    die(1).start()
    held = pl.ds(pl.multiple_of(OWN * EXPERTS * c, 8), OWN * EXPERTS)
    my_m = [pltpu.make_async_copy(
        mom.at[:, pl.ds(LANES * n, LANES)], mm.at[n, held], m_l.at[n]) for n in range(D // LANES)]
    his_m = [remote(mom.at[:, pl.ds(LANES * n, LANES)], mm.at[n, held], m_s.at[n], m_r.at[n], sib)
             for n in range(D // LANES)]
    for cp in my_m + his_m:
        cp.start()

    half = MINE // 2
    lower, upper = pl.ds(0, half), pl.ds(half, half)

    ringed = ROUNDS - DIRECT
    phases = ((stage, r1a, r2a, (a1, a2, a3), an, ap), (p2, r1b, r2b, (b1, b2, b3), bn, bp))

    def first(f, q):
        src, r1, _, (_, far, _), following, previous = phases[f]
        return (remote(src.at[q, far, lower], r1.at[q, 0], s1_s.at[f, q, 0], s1_r.at[f, q, 0],
                       following),
                remote(src.at[q, far, upper], r1.at[q, 1], s1_s.at[f, q, 1], s1_r.at[f, q, 1],
                       previous))

    def alone(f, q):
        src, _, r2, (near, _, back), following, previous = phases[f]
        return (remote(src.at[q, near, upper], r2.at[q, 0, upper], h_s.at[f, q, 0],
                       h_r.at[f, q, 0], following),
                remote(src.at[q, back, lower], r2.at[q, 1, lower], h_s.at[f, q, 1],
                       h_r.at[f, q, 1], previous))

    def second(f, q):
        src, _, r2, (near, _, back), following, previous = phases[f]
        return (remote(src.at[q, near, lower], r2.at[q, 0, lower], s2_s.at[f, q, 0],
                       s2_r.at[f, q, 0], following),
                remote(src.at[q, back, upper], r2.at[q, 1, upper], s2_s.at[f, q, 1],
                       s2_r.at[f, q, 1], previous))

    def third(q):
        d = q - ringed
        return [remote(p2.at[q, t], r3.at[d, i], p_s.at[d, i], p_r.at[d, i], dev)
                for i, (t, dev) in enumerate(((b1, bn), (b3, bp), (b2, bo)))]

    def do_die(q):
        if q + 2 < ROUNDS:
            die(q + 2).start()
            load(q + 2).start()
        load(q).wait()
        die(q).wait_recv()

        @pl.when(c == 1)
        def _():
            def one(e, _):
                for k in range(SIDE):
                    rows = pl.ds(QUARTER * k, QUARTER)
                    stage[q, k, e] = own[q, e, rows, :] + got[q, e, rows, :]
                return 0

            lax.fori_loop(0, MINE, one, 0)

        @pl.when(c == 0)
        def _():
            def one(e, _):
                for k in range(CHIPS):
                    rows = pl.ds(ROWS * k, ROWS)
                    stage[q, k % SIDE, e, pl.ds(ROWS * (k // SIDE), ROWS), :] = (
                        own[q, e, rows, :] + got[q, e, rows, :])
                return 0

            lax.fori_loop(0, MINE, one, 0)

        for cp in first(0, q) + alone(0, q):
            cp.start()

    def do_mid(f, q):
        src, r1, _, (near, _, back), _, _ = phases[f]
        for side, (tgt, lo) in enumerate(((near, 0), (back, half))):
            first(f, q)[side].wait_recv()

            def one(e, _):
                src[q, tgt, lo + e] = src[q, tgt, lo + e] + r1[q, side, e]
                return 0

            lax.fori_loop(0, half, one, 0)
            second(f, q)[side].start()

    def do_sum(q):
        for cp in alone(0, q) + second(0, q):
            cp.wait_recv()

        def one(e, _):
            total = stage[q, a, e].astype(jnp.float32) + r2a[q, 0, e].astype(jnp.float32)
            total = total + r2a[q, 1, e].astype(jnp.float32)
            for k in range(SIDE):
                p2[q, k, e, pl.ds(0, ROWS), :] = (
                    total[ROWS * k:ROWS * (k + 1)].astype(jnp.bfloat16))
            return 0

        lax.fori_loop(0, MINE, one, 0)
        for cp in third(q) if q >= ringed else first(1, q) + alone(1, q):
            cp.start()

    def owner(e):
        oy = e // 2
        ox = oy % 2 + 2 * (e % 2)
        return oy, ox, (oy * SIDE + ox) * 2 + e // MINE

    chip = me // 2
    here = pl.ds(pl.multiple_of(SLOT * chip, 16), SLOT)

    def gather(q, j, dev):
        return remote(bl.at[q, j], xa.at[here, cols(q)], g_s.at[q, j], g_r.at[q], (dev, z))

    def gather_own(q, j):
        return pltpu.make_async_copy(bl.at[q, j], xa.at[here, cols(q)], g_r.at[q])

    def gather_row(q, j, oy):
        row = (y - oy) % SIDE - 1
        return remote(bl.at[q, j], rb.at[q, row], g_s.at[q, j], b_r.at[q, row],
                      ((oy * SIDE + x) * 2 + c, z))

    def relay(q, row):
        there = pl.ds(pl.multiple_of(SLOT * (((y + row + 1) % SIDE) * SIDE + x), 16), SLOT)
        dev = (y * SIDE + y % 2 + 2 * (q % 2)) * 2 + c
        return remote(rb.at[q, row], xa.at[there, cols(q)], b_s.at[q, row], g_r.at[q], (dev, z))

    def relays(q):
        return (c == y // 2) & (x != y % 2 + 2 * (q % 2))

    def do_relay(q):
        @pl.when(relays(q))
        def _():
            for row in range(SIDE - 1):
                landed = rb.at[q, row]
                pltpu.make_async_copy(landed, landed, b_r.at[q, row]).wait()
                relay(q, row).start()

    real = lax.broadcasted_iota(jnp.int32, (SLOT, W), 0) < ROWS

    def do_blend(q):
        for cp in third(q) if q >= ringed else alone(1, q) + second(1, q):
            cp.wait_recv()
        came = ([r3.at[q - ringed, i] for i in range(3)] if q >= ringed
                else [r2b.at[q, i] for i in range(2)])
        if q == 0:
            for cp in my_m + his_m:
                cp.wait()

        def one(j, _):
            total = p2[q, b, j].astype(jnp.float32)
            for ref in came:
                total = total + ref[j].astype(jnp.float32)
            turns = range(q * W // LANES, (q + 1) * W // LANES)
            these = pl.ds(MINE * c + j, SLOT, stride=EXPERTS)
            before = jnp.concatenate([mm[n, these, :] for n in turns], axis=1)
            after = BETA * before + total
            for i, n in enumerate(turns):
                mm[n, these, :] = after[:, i * LANES:(i + 1) * LANES]
            bl[q, j] = jnp.where(real, total + BETA * after, 0.0).astype(jnp.bfloat16)
            oy, ox, there = owner(MINE * c + j)
            turned = (x != ox) & (y != oy) & (j % 2 == q % 2) if q < RELAYED else False

            @pl.when(there == me)
            def _():
                gather_own(q, j).start()

            @pl.when((there != me) & jnp.logical_not(turned))
            def _():
                gather(q, j, there).start()

            if q < RELAYED:
                @pl.when(turned)
                def _():
                    gather_row(q, j, oy).start()

            return 0

        lax.fori_loop(0, MINE, one, 0)

    end = ROUNDS + 1
    steps = []
    for q in range(ROUNDS):
        steps += [(q, 0, q, do_die), (q + 1, 1, q, functools.partial(do_mid, 0)),
                  (min(q + LAG, end), 2, q, do_sum)]
        if q < ringed:
            steps.append((min(q + LAG + 1, end), 3, q, functools.partial(do_mid, 1)))
        steps.append((min(q + LAG + (2 if q < ringed else 1), end), 4, q, do_blend))
        if q < RELAYED:
            steps.append((min(q + LAG + 3, end), 5, q, do_relay))
    for _, _, q, step in sorted(steps, key=lambda item: item[:3]):
        step(q)

    def share(core):
        return pl.ds(pl.multiple_of(OWN * EXPERTS * core, 8), OWN * EXPERTS)

    my_mo = [pltpu.make_async_copy(
        mm.at[n, share(c)], mo_out.at[:, pl.ds(LANES * n, LANES)], mo_l.at[n])
        for n in range(D // LANES)]
    his_mo = [remote(mm.at[n, share(1 - c)], ms.at[n], mo_s.at[n], mo_r.at[n], sib)
              for n in range(D // LANES)]
    for cp in his_mo:
        cp.start()

    def finish_mo():
        row = lax.broadcasted_iota(jnp.int32, (OWN * EXPERTS, LANES), 0)
        ours = (row % EXPERTS) // MINE == c
        for n in range(D // LANES):
            his_mo[n].wait_recv()
            mm[n, share(c), :] = jnp.where(ours, mm[n, share(c), :], ms[n])
            my_mo[n].start()

    oy = x % 2 + 2 * c
    mine = 2 * oy + x // 2
    right = pl.ds(LEFT, D - LEFT)

    def left(part):
        return pl.ds(PART * part, PART)

    def give_row(part, d):
        row = (oy + d) % SIDE
        rows = pl.ds(pl.multiple_of(SIDE * SLOT * row, 16), SIDE * SLOT)
        return remote(up.at[rows, left(part)], lb.at[part], l_s.at[part, d - 1], l_r.at[part],
                      ((row * SIDE + x) * 2 + c, z))

    def give(dev):
        rows = pl.ds(pl.multiple_of(SLOT * (dev // 2) + 16 * (dev % 2), 16), 32)
        return remote(up.at[rows, right], up_out.at[mine, :, right], u_s.at[dev], u_r, (dev, z))

    def give_own():
        rows = pl.ds(pl.multiple_of(SLOT * chip + 16 * c, 16), 32)
        return pltpu.make_async_copy(up.at[rows, right], up_out.at[mine, :, right], u_r)

    def spread(src, base, part, n):
        dev = (y * SIDE) * 2 + n
        rows = pl.ds(pl.multiple_of(base + SLOT * (n // 2) + 16 * (n % 2), 16), 32)
        return remote(src.at[rows], up_out.at[mine, :, left(part)], v_s.at[part, n], u_r, (dev, z))

    def spread_all(src, base, part):
        def one(n, _):
            @pl.when(y * SIDE * 2 + n != me)
            def _():
                spread(src, base, part, n).start()
            return 0

        lax.fori_loop(0, 2 * SIDE, one, 0)
        rows = pl.ds(pl.multiple_of(base + SLOT * x + 16 * c, 16), 32)
        pltpu.make_async_copy(src.at[rows], up_out.at[mine, :, left(part)], u_r).start()

    @pl.when(y == oy)
    def _():
        blocks = [slice(i * BLOCK, (i + 1) * BLOCK) for i in range(TALL // BLOCK)]
        strips = [slice(i * STRIP, (i + 1) * STRIP) for i in range(TALL // STRIP)]
        pairs = [(rows, others) for i, rows in enumerate(blocks) for others in blocks[i:]]

        def arrived(q):
            pltpu.make_async_copy(xa.at[:, cols(q)], xa.at[:, cols(q)], g_r.at[q]).wait()

        def products(rows, others, part, matrix):
            return lax.dot_general(
                matrix[rows, part], matrix[others, part], (((1,), (1,)), ((), ())),
                preferred_element_type=jnp.float32)

        def squares(part):
            total = jnp.zeros((1, part.stop - part.start), jnp.float32)
            for rows in strips:
                v = xa[rows, part].astype(jnp.float32)
                total = total + jnp.sum(v * v, axis=0, keepdims=True)
            return jnp.sum(total, axis=1, keepdims=True)

        def put(rows, others, block):
            gb[rows, others] = block.astype(jnp.bfloat16)
            if others.start > rows.start:
                gb[others, rows] = block.T.astype(jnp.bfloat16)

        head, tail = slice(0, EARLY * W), slice(EARLY * W, D)
        for q in range(EARLY):
            arrived(q)
        for rows, others in pairs:
            ga[rows, others] = products(rows, others, head, xa)
        norm = squares(head)
        for q in range(EARLY, ROUNDS):
            arrived(q)
        norm = jnp.sqrt(norm + squares(tail))
        scale = 1.0 / (norm + EPS)
        for rows, others in pairs:
            block = ga[rows, others] + products(rows, others, tail, xa)
            put(rows, others, block * (scale * scale))
        for rows in strips:
            xa[rows, :] = (xa[rows, :].astype(jnp.float32) * scale).astype(jnp.bfloat16)

        src, dst = xa, xb
        for turn in range(ITERS):
            if turn > 0:
                for rows, others in pairs:
                    put(rows, others, products(rows, others, slice(0, D), src))
            for rows, others in pairs:
                squared = jnp.dot(gb[rows, :], gb[:, others], preferred_element_type=jnp.float32)
                poly = (B * gb[rows, others].astype(jnp.float32) + C * squared).astype(
                    jnp.bfloat16)
                pb[rows, others] = poly
                if others.start > rows.start:
                    pb[others, rows] = poly.T
            if turn < ITERS - 1:
                for rows in strips:
                    mixed = jnp.dot(pb[rows, :], src[...], preferred_element_type=jnp.float32)
                    dst[rows, :] = (A * src[rows, :].astype(jnp.float32) + mixed).astype(
                        jnp.bfloat16)
                src, dst = dst, src
                continue
            for part in range(PARTS + 1):
                these = slice(PART * part, PART * (part + 1) if part < PARTS else D)
                for rows in strips:
                    mixed = jnp.dot(pb[rows, :], src[:, these], preferred_element_type=jnp.float32)
                    new = (A * src[rows, these].astype(jnp.float32) + mixed).astype(jnp.bfloat16)
                    up[rows, these] = (new.astype(jnp.float32) * 32.0).astype(jnp.bfloat16)
                if part < PARTS:
                    for d in (2, 1, 3):
                        give_row(part, d).start()
                    spread_all(up.at[:, left(part)], SIDE * SLOT * y, part)

        def send(dev, _):
            @pl.when(dev != me)
            def _():
                give(dev).start()
            return 0

        lax.fori_loop(0, 2 * CHIPS, send, 0)
        give_own().start()
        finish_mo()

        def sent(dev, _):
            @pl.when(dev != me)
            def _():
                give(dev).wait_send()
            return 0

        lax.fori_loop(0, 2 * CHIPS, sent, 0)
        for part in range(PARTS):
            for d in range(1, SIDE):
                give_row(part, d).wait_send()

    @pl.when(y != oy)
    def _():
        finish_mo()
        for part in range(PARTS):
            give_row(part, 1).wait_recv()
            spread_all(lb.at[part], 0, part)

    for q in range(ROUNDS):
        die(q).wait_send()
        for f in range(2):
            if f == 0 or q < ringed:
                for cp in first(f, q) + alone(f, q) + second(f, q):
                    cp.wait_send()
        if q >= ringed:
            for cp in third(q):
                cp.wait_send()

        def sent(j, _, q=q):
            @pl.when(owner(MINE * c + j)[2] != me)
            def _():
                gather(q, j, sib[0]).wait_send()
            return 0

        lax.fori_loop(0, MINE, sent, 0)
        if q < RELAYED:
            @pl.when(relays(q))
            def _(q=q):
                for row in range(SIDE - 1):
                    relay(q, row).wait_send()
    for n in range(D // LANES):
        his_mo[n].wait_send()
        my_mo[n].wait()

    for part in range(PARTS):
        def spread_sent(n, _, part=part):
            @pl.when(y * SIDE * 2 + n != me)
            def _():
                spread(lb.at[part], 0, part, n).wait_send()
            return 0

        lax.fori_loop(0, 2 * SIDE, spread_sent, 0)
    pltpu.make_async_copy(up_out, up_out, u_r).wait()


def reduce_and_step(grads, mom):
    bf, f32 = jnp.bfloat16, jnp.float32
    dma = pltpu.SemaphoreType.DMA
    half = MINE // 2
    tiles = D // LANES
    return pl.pallas_call(
        kernel,
        out_shape=(
            jax.ShapeDtypeStruct((OWN * EXPERTS, D), f32),
            jax.ShapeDtypeStruct((EXPERTS, 32, D), bf),
        ),
        in_specs=[pl.BlockSpec(memory_space=pl.ANY)] * 2,
        out_specs=(pl.BlockSpec(memory_space=pl.ANY),) * 2,
        scratch_shapes=[
            pltpu.VMEM((ROUNDS, MINE, HID, W), bf),
            pltpu.VMEM((ROUNDS, MINE, HID, W), bf),
            pltpu.VMEM((ROUNDS, SIDE, MINE, QUARTER, W), bf),
            pltpu.VMEM((ROUNDS, 2, half, QUARTER, W), bf),
            pltpu.VMEM((ROUNDS, 2, MINE, QUARTER, W), bf),
            pltpu.VMEM((ROUNDS, SIDE, MINE, SLOT, W), bf),
            pltpu.VMEM((ROUNDS, 2, half, SLOT, W), bf),
            pltpu.VMEM((ROUNDS, 2, MINE, SLOT, W), bf),
            pltpu.VMEM((DIRECT, 3, MINE, SLOT, W), bf),
            pltpu.VMEM((ROUNDS, MINE, SLOT, W), bf),
            pltpu.VMEM((tiles, SLOT * EXPERTS, LANES), f32),
            pltpu.VMEM((tiles, OWN * EXPERTS, LANES), f32),
            pltpu.VMEM((TALL, D), bf),
            pltpu.VMEM((TALL, D), bf),
            pltpu.VMEM((TALL, TALL), f32),
            pltpu.VMEM((TALL, TALL), bf),
            pltpu.VMEM((TALL, TALL), bf),
            pltpu.VMEM((TALL, D), bf),
            pltpu.VMEM((RELAYED, SIDE - 1, SLOT, W), bf),
            pltpu.VMEM((PARTS, SIDE * SLOT, PART), bf),
            dma((ROUNDS,)), dma((ROUNDS,)), dma((ROUNDS,)),
            dma((2, ROUNDS, 2)), dma((2, ROUNDS, 2)),
            dma((2, ROUNDS, 2)), dma((2, ROUNDS, 2)),
            dma((2, ROUNDS, 2)), dma((2, ROUNDS, 2)),
            dma((DIRECT, 3)), dma((DIRECT, 3)),
            dma((ROUNDS, MINE)), dma((ROUNDS,)),
            dma((RELAYED, SIDE - 1)), dma((RELAYED, SIDE - 1)),
            dma((tiles,)), dma((tiles,)), dma((tiles,)),
            dma((tiles,)), dma((tiles,)), dma((tiles,)),
            dma((PARTS, SIDE - 1)), dma((PARTS,)),
            dma((PARTS, 2 * SIDE)),
            dma((2 * CHIPS,)), dma(()),
        ],
        compiler_params=pltpu.CompilerParams(
            collective_id=0, has_side_effects=True, vmem_limit_bytes=209 * 2**18),
        name="muon",
    )(grads, mom)


def per_device(grads, momentum):
    c = lax.axis_index("dp") % 2
    mom = jnp.transpose(momentum, (1, 0, 2)).reshape(OWN * EXPERTS, D)
    mo, up = reduce_and_step(grads[0], mom)
    mo = jnp.transpose(mo.reshape(OWN, EXPERTS, D), (1, 0, 2))
    return mo, lax.dynamic_slice_in_dim(up, (OWN - 16) * c, OWN, 1)


def solution(mesh):
    return jax.shard_map(
        per_device,
        mesh=mesh,
        in_specs=(P("dp", "expert", None, None), P("expert", "dp", None)),
        out_specs=(P("expert", "dp", None), P("expert", "dp", None)),
        check_vma=False,
    )
```

```python
import functools

import jax
import jax.numpy as jnp
from jax import lax
from jax.experimental import pallas as pl
from jax.experimental.pallas import tpu as pltpu
from jax.sharding import PartitionSpec as P

MESH = pl.DeviceIdType.MESH
ITERS = 3
A, B, C = 3.4445, -4.775, 2.0315
BETA = 0.95
EPS = 1e-07

SIDE = 4
CHIPS = SIDE * SIDE
EXPERTS = 8
MINE = 4
HID, D = 704, 1024
ROWS = HID // CHIPS
SLOT = 48
QUARTER = HID // SIDE
OWN = HID // (2 * CHIPS)
ROUNDS = 8
LAG = 5
DIRECT = 3
RELAYED = 2
W = D // ROUNDS
TALL = CHIPS * SLOT
LANES = 128
LEFT = 512
PARTS = 2
PART = LEFT // PARTS
BLOCK = 256
STRIP = 128
EARLY = 6


def kernel(grads, mom, mo_out, up_out, own, got, stage, r1a, r2a, p2, r1b, r2b, r3, bl, mm, ms,
           xa, xb, ga, gb, pb, up, rb, lb, own_s, die_ss, die_rs, s1_s, s1_r, s2_s, s2_r, h_s, h_r,
           p_s, p_r, g_s, g_r, b_s, b_r, m_l, m_s, m_r, mo_l, mo_s, mo_r, l_s, l_r, v_s, u_s, u_r):
    me = lax.axis_index("dp")
    z = lax.axis_index("expert")
    c = me % 2
    x = (me // 2) % SIDE
    y = me // (2 * SIDE)
    a = jnp.where(c == 0, x, y)
    b = jnp.where(c == 0, y, x)

    def at(a_, b_):
        a_, b_ = a_ % SIDE, b_ % SIDE
        row = jnp.where(c == 0, b_, a_)
        col = jnp.where(c == 0, a_, b_)
        return ((row * SIDE + col) * 2 + c, z)

    sib = (me + 1 - 2 * c, z)
    an, ap = at(a + 1, b), at(a + 3, b)
    bn, bp, bo = at(a, b + 1), at(a, b + 3), at(a, b + 2)
    a1, a2, a3 = (a + 1) % SIDE, (a + 2) % SIDE, (a + 3) % SIDE
    b1, b2, b3 = (b + 1) % SIDE, (b + 2) % SIDE, (b + 3) % SIDE

    def remote(src, dst, ss, rs, dev):
        return pltpu.make_async_remote_copy(
            src, dst, ss, rs, device_id=dev, device_id_type=MESH)

    def cols(q):
        return pl.ds(q * W, W)

    def load(q):
        return pltpu.make_async_copy(
            grads.at[pl.ds(MINE * c, MINE), :, cols(q)], own.at[q], own_s.at[q])

    load(0).start()
    load(1).start()

    barrier = pltpu.get_barrier_semaphore()
    for dev in (sib, an, ap, bn, bp, bo):
        pl.semaphore_signal(barrier, inc=1, device_id=dev, device_id_type=MESH)
    pl.semaphore_wait(barrier, 6)

    def die(q):
        return remote(grads.at[pl.ds(MINE * (1 - c), MINE), :, cols(q)], got.at[q],
                      die_ss.at[q], die_rs.at[q], sib)

    die(0).start()
    die(1).start()
    held = pl.ds(pl.multiple_of(OWN * EXPERTS * c, 8), OWN * EXPERTS)
    my_m = [pltpu.make_async_copy(
        mom.at[:, pl.ds(LANES * n, LANES)], mm.at[n, held], m_l.at[n]) for n in range(D // LANES)]
    his_m = [remote(mom.at[:, pl.ds(LANES * n, LANES)], mm.at[n, held], m_s.at[n], m_r.at[n], sib)
             for n in range(D // LANES)]
    for cp in my_m + his_m:
        cp.start()

    half = MINE // 2
    lower, upper = pl.ds(0, half), pl.ds(half, half)

    ringed = ROUNDS - DIRECT
    phases = ((stage, r1a, r2a, (a1, a2, a3), an, ap), (p2, r1b, r2b, (b1, b2, b3), bn, bp))

    def first(f, q):
        src, r1, _, (_, far, _), following, previous = phases[f]
        return (remote(src.at[q, far, lower], r1.at[q, 0], s1_s.at[f, q, 0], s1_r.at[f, q, 0],
                       following),
                remote(src.at[q, far, upper], r1.at[q, 1], s1_s.at[f, q, 1], s1_r.at[f, q, 1],
                       previous))

    def alone(f, q):
        src, _, r2, (near, _, back), following, previous = phases[f]
        return (remote(src.at[q, near, upper], r2.at[q, 0, upper], h_s.at[f, q, 0],
                       h_r.at[f, q, 0], following),
                remote(src.at[q, back, lower], r2.at[q, 1, lower], h_s.at[f, q, 1],
                       h_r.at[f, q, 1], previous))

    def second(f, q):
        src, _, r2, (near, _, back), following, previous = phases[f]
        return (remote(src.at[q, near, lower], r2.at[q, 0, lower], s2_s.at[f, q, 0],
                       s2_r.at[f, q, 0], following),
                remote(src.at[q, back, upper], r2.at[q, 1, upper], s2_s.at[f, q, 1],
                       s2_r.at[f, q, 1], previous))

    def third(q):
        d = q - ringed
        return [remote(p2.at[q, t], r3.at[d, i], p_s.at[d, i], p_r.at[d, i], dev)
                for i, (t, dev) in enumerate(((b1, bn), (b3, bp), (b2, bo)))]

    def do_die(q):
        if q + 2 < ROUNDS:
            die(q + 2).start()
            load(q + 2).start()
        load(q).wait()
        die(q).wait_recv()

        @pl.when(c == 1)
        def _():
            def one(e, _):
                for k in range(SIDE):
                    rows = pl.ds(QUARTER * k, QUARTER)
                    stage[q, k, e] = own[q, e, rows, :] + got[q, e, rows, :]
                return 0

            lax.fori_loop(0, MINE, one, 0)

        @pl.when(c == 0)
        def _():
            def one(e, _):
                for k in range(CHIPS):
                    rows = pl.ds(ROWS * k, ROWS)
                    stage[q, k % SIDE, e, pl.ds(ROWS * (k // SIDE), ROWS), :] = (
                        own[q, e, rows, :] + got[q, e, rows, :])
                return 0

            lax.fori_loop(0, MINE, one, 0)

        for cp in first(0, q) + alone(0, q):
            cp.start()

    def do_mid(f, q):
        src, r1, _, (near, _, back), _, _ = phases[f]
        for side, (tgt, lo) in enumerate(((near, 0), (back, half))):
            first(f, q)[side].wait_recv()

            def one(e, _):
                src[q, tgt, lo + e] = src[q, tgt, lo + e] + r1[q, side, e]
                return 0

            lax.fori_loop(0, half, one, 0)
            second(f, q)[side].start()

    def do_sum(q):
        for cp in alone(0, q) + second(0, q):
            cp.wait_recv()

        def one(e, _):
            total = stage[q, a, e].astype(jnp.float32) + r2a[q, 0, e].astype(jnp.float32)
            total = total + r2a[q, 1, e].astype(jnp.float32)
            for k in range(SIDE):
                p2[q, k, e, pl.ds(0, ROWS), :] = (
                    total[ROWS * k:ROWS * (k + 1)].astype(jnp.bfloat16))
            return 0

        lax.fori_loop(0, MINE, one, 0)
        for cp in third(q) if q >= ringed else first(1, q) + alone(1, q):
            cp.start()

    def owner(e):
        oy = e // 2
        ox = oy % 2 + 2 * (e % 2)
        return oy, ox, (oy * SIDE + ox) * 2 + e // MINE

    chip = me // 2
    here = pl.ds(pl.multiple_of(SLOT * chip, 16), SLOT)

    def gather(q, j, dev):
        return remote(bl.at[q, j], xa.at[here, cols(q)], g_s.at[q, j], g_r.at[q], (dev, z))

    def gather_own(q, j):
        return pltpu.make_async_copy(bl.at[q, j], xa.at[here, cols(q)], g_r.at[q])

    def gather_row(q, j, oy):
        row = (y - oy) % SIDE - 1
        return remote(bl.at[q, j], rb.at[q, row], g_s.at[q, j], b_r.at[q, row],
                      ((oy * SIDE + x) * 2 + c, z))

    def relay(q, row):
        there = pl.ds(pl.multiple_of(SLOT * (((y + row + 1) % SIDE) * SIDE + x), 16), SLOT)
        dev = (y * SIDE + y % 2 + 2 * (q % 2)) * 2 + c
        return remote(rb.at[q, row], xa.at[there, cols(q)], b_s.at[q, row], g_r.at[q], (dev, z))

    def relays(q):
        return (c == y // 2) & (x != y % 2 + 2 * (q % 2))

    def do_relay(q):
        @pl.when(relays(q))
        def _():
            for row in range(SIDE - 1):
                landed = rb.at[q, row]
                pltpu.make_async_copy(landed, landed, b_r.at[q, row]).wait()
                relay(q, row).start()

    real = lax.broadcasted_iota(jnp.int32, (SLOT, W), 0) < ROWS

    def do_blend(q):
        for cp in third(q) if q >= ringed else alone(1, q) + second(1, q):
            cp.wait_recv()
        came = ([r3.at[q - ringed, i] for i in range(3)] if q >= ringed
                else [r2b.at[q, i] for i in range(2)])
        if q == 0:
            for cp in my_m + his_m:
                cp.wait()

        def one(j, _):
            total = p2[q, b, j].astype(jnp.float32)
            for ref in came:
                total = total + ref[j].astype(jnp.float32)
            turns = range(q * W // LANES, (q + 1) * W // LANES)
            these = pl.ds(MINE * c + j, SLOT, stride=EXPERTS)
            before = jnp.concatenate([mm[n, these, :] for n in turns], axis=1)
            after = BETA * before + total
            for i, n in enumerate(turns):
                mm[n, these, :] = after[:, i * LANES:(i + 1) * LANES]
            bl[q, j] = jnp.where(real, total + BETA * after, 0.0).astype(jnp.bfloat16)
            oy, ox, there = owner(MINE * c + j)
            turned = (x != ox) & (y != oy) & (j % 2 == q % 2) if q < RELAYED else False

            @pl.when(there == me)
            def _():
                gather_own(q, j).start()

            @pl.when((there != me) & jnp.logical_not(turned))
            def _():
                gather(q, j, there).start()

            if q < RELAYED:
                @pl.when(turned)
                def _():
                    gather_row(q, j, oy).start()

            return 0

        lax.fori_loop(0, MINE, one, 0)

    end = ROUNDS + 1
    steps = []
    for q in range(ROUNDS):
        steps += [(q, 0, q, do_die), (q + 1, 1, q, functools.partial(do_mid, 0)),
                  (min(q + LAG, end), 2, q, do_sum)]
        if q < ringed:
            steps.append((min(q + LAG + 1, end), 3, q, functools.partial(do_mid, 1)))
        steps.append((min(q + LAG + (2 if q < ringed else 1), end), 4, q, do_blend))
        if q < RELAYED:
            steps.append((min(q + LAG + 3, end), 5, q, do_relay))
    for _, _, q, step in sorted(steps, key=lambda item: item[:3]):
        step(q)

    def share(core):
        return pl.ds(pl.multiple_of(OWN * EXPERTS * core, 8), OWN * EXPERTS)

    my_mo = [pltpu.make_async_copy(
        mm.at[n, share(c)], mo_out.at[:, pl.ds(LANES * n, LANES)], mo_l.at[n])
        for n in range(D // LANES)]
    his_mo = [remote(mm.at[n, share(1 - c)], ms.at[n], mo_s.at[n], mo_r.at[n], sib)
              for n in range(D // LANES)]
    for cp in his_mo:
        cp.start()

    def finish_mo():
        row = lax.broadcasted_iota(jnp.int32, (OWN * EXPERTS, LANES), 0)
        ours = (row % EXPERTS) // MINE == c
        for n in range(D // LANES):
            his_mo[n].wait_recv()
            mm[n, share(c), :] = jnp.where(ours, mm[n, share(c), :], ms[n])
            my_mo[n].start()

    oy = x % 2 + 2 * c
    mine = 2 * oy + x // 2
    right = pl.ds(LEFT, D - LEFT)

    def left(part):
        return pl.ds(PART * part, PART)

    def give_row(part, d):
        row = (oy + d) % SIDE
        rows = pl.ds(pl.multiple_of(SIDE * SLOT * row, 16), SIDE * SLOT)
        return remote(up.at[rows, left(part)], lb.at[part], l_s.at[part, d - 1], l_r.at[part],
                      ((row * SIDE + x) * 2 + c, z))

    def give(dev):
        rows = pl.ds(pl.multiple_of(SLOT * (dev // 2) + 16 * (dev % 2), 16), 32)
        return remote(up.at[rows, right], up_out.at[mine, :, right], u_s.at[dev], u_r, (dev, z))

    def give_own():
        rows = pl.ds(pl.multiple_of(SLOT * chip + 16 * c, 16), 32)
        return pltpu.make_async_copy(up.at[rows, right], up_out.at[mine, :, right], u_r)

    def spread(src, base, part, n):
        dev = (y * SIDE) * 2 + n
        rows = pl.ds(pl.multiple_of(base + SLOT * (n // 2) + 16 * (n % 2), 16), 32)
        return remote(src.at[rows], up_out.at[mine, :, left(part)], v_s.at[part, n], u_r, (dev, z))

    def spread_all(src, base, part):
        def one(n, _):
            spread(src, base, part, (2 * x + c + n) % (2 * SIDE)).start()
            return 0

        lax.fori_loop(1, 2 * SIDE, one, 0)
        rows = pl.ds(pl.multiple_of(base + SLOT * x + 16 * c, 16), 32)
        pltpu.make_async_copy(src.at[rows], up_out.at[mine, :, left(part)], u_r).start()

    @pl.when(y == oy)
    def _():
        blocks = [slice(i * BLOCK, (i + 1) * BLOCK) for i in range(TALL // BLOCK)]
        strips = [slice(i * STRIP, (i + 1) * STRIP) for i in range(TALL // STRIP)]
        pairs = [(rows, others) for i, rows in enumerate(blocks) for others in blocks[i:]]

        def arrived(q):
            pltpu.make_async_copy(xa.at[:, cols(q)], xa.at[:, cols(q)], g_r.at[q]).wait()

        def products(rows, others, part, matrix):
            return lax.dot_general(
                matrix[rows, part], matrix[others, part], (((1,), (1,)), ((), ())),
                preferred_element_type=jnp.float32)

        def squares(part):
            total = jnp.zeros((1, part.stop - part.start), jnp.float32)
            for rows in strips:
                v = xa[rows, part].astype(jnp.float32)
                total = total + jnp.sum(v * v, axis=0, keepdims=True)
            return jnp.sum(total, axis=1, keepdims=True)

        def put(rows, others, block):
            gb[rows, others] = block.astype(jnp.bfloat16)
            if others.start > rows.start:
                gb[others, rows] = block.T.astype(jnp.bfloat16)

        head, tail = slice(0, EARLY * W), slice(EARLY * W, D)
        for q in range(EARLY):
            arrived(q)
        for rows, others in pairs:
            ga[rows, others] = products(rows, others, head, xa)
        norm = squares(head)
        for q in range(EARLY, ROUNDS):
            arrived(q)
        norm = jnp.sqrt(norm + squares(tail))
        scale = 1.0 / (norm + EPS)
        for rows, others in pairs:
            block = ga[rows, others] + products(rows, others, tail, xa)
            put(rows, others, block * (scale * scale))
        for rows in strips:
            xa[rows, :] = (xa[rows, :].astype(jnp.float32) * scale).astype(jnp.bfloat16)

        src, dst = xa, xb
        for turn in range(ITERS):
            if turn > 0:
                for rows, others in pairs:
                    put(rows, others, products(rows, others, slice(0, D), src))
            for rows, others in pairs:
                squared = jnp.dot(gb[rows, :], gb[:, others], preferred_element_type=jnp.float32)
                poly = (B * gb[rows, others].astype(jnp.float32) + C * squared).astype(
                    jnp.bfloat16)
                pb[rows, others] = poly
                if others.start > rows.start:
                    pb[others, rows] = poly.T
            if turn < ITERS - 1:
                for rows in strips:
                    mixed = jnp.dot(pb[rows, :], src[...], preferred_element_type=jnp.float32)
                    dst[rows, :] = (A * src[rows, :].astype(jnp.float32) + mixed).astype(
                        jnp.bfloat16)
                src, dst = dst, src
                continue
            for part in range(PARTS + 1):
                these = slice(PART * part, PART * (part + 1) if part < PARTS else D)
                for rows in strips:
                    mixed = jnp.dot(pb[rows, :], src[:, these], preferred_element_type=jnp.float32)
                    new = (A * src[rows, these].astype(jnp.float32) + mixed).astype(jnp.bfloat16)
                    up[rows, these] = (new.astype(jnp.float32) * 32.0).astype(jnp.bfloat16)
                if part < PARTS:
                    for d in (2, 1, 3):
                        give_row(part, d).start()
                    spread_all(up.at[:, left(part)], SIDE * SLOT * y, part)

        def send(dev, _):
            @pl.when(dev != me)
            def _():
                give(dev).start()
            return 0

        lax.fori_loop(0, 2 * CHIPS, send, 0)
        give_own().start()
        finish_mo()

        def sent(dev, _):
            @pl.when(dev != me)
            def _():
                give(dev).wait_send()
            return 0

        lax.fori_loop(0, 2 * CHIPS, sent, 0)
        for part in range(PARTS):
            for d in range(1, SIDE):
                give_row(part, d).wait_send()

    @pl.when(y != oy)
    def _():
        finish_mo()
        for part in range(PARTS):
            give_row(part, 1).wait_recv()
            spread_all(lb.at[part], 0, part)

    for q in range(ROUNDS):
        die(q).wait_send()
        for f in range(2):
            if f == 0 or q < ringed:
                for cp in first(f, q) + alone(f, q) + second(f, q):
                    cp.wait_send()
        if q >= ringed:
            for cp in third(q):
                cp.wait_send()

        def sent(j, _, q=q):
            @pl.when(owner(MINE * c + j)[2] != me)
            def _():
                gather(q, j, sib[0]).wait_send()
            return 0

        lax.fori_loop(0, MINE, sent, 0)
        if q < RELAYED:
            @pl.when(relays(q))
            def _(q=q):
                for row in range(SIDE - 1):
                    relay(q, row).wait_send()
    for n in range(D // LANES):
        his_mo[n].wait_send()
        my_mo[n].wait()

    for part in range(PARTS):
        def spread_sent(n, _, part=part):
            @pl.when(y * SIDE * 2 + n != me)
            def _():
                spread(lb.at[part], 0, part, n).wait_send()
            return 0

        lax.fori_loop(0, 2 * SIDE, spread_sent, 0)
    pltpu.make_async_copy(up_out, up_out, u_r).wait()


def reduce_and_step(grads, mom):
    bf, f32 = jnp.bfloat16, jnp.float32
    dma = pltpu.SemaphoreType.DMA
    half = MINE // 2
    tiles = D // LANES
    return pl.pallas_call(
        kernel,
        out_shape=(
            jax.ShapeDtypeStruct((OWN * EXPERTS, D), f32),
            jax.ShapeDtypeStruct((EXPERTS, 32, D), bf),
        ),
        in_specs=[pl.BlockSpec(memory_space=pl.ANY)] * 2,
        out_specs=(pl.BlockSpec(memory_space=pl.ANY),) * 2,
        scratch_shapes=[
            pltpu.VMEM((ROUNDS, MINE, HID, W), bf),
            pltpu.VMEM((ROUNDS, MINE, HID, W), bf),
            pltpu.VMEM((ROUNDS, SIDE, MINE, QUARTER, W), bf),
            pltpu.VMEM((ROUNDS, 2, half, QUARTER, W), bf),
            pltpu.VMEM((ROUNDS, 2, MINE, QUARTER, W), bf),
            pltpu.VMEM((ROUNDS, SIDE, MINE, SLOT, W), bf),
            pltpu.VMEM((ROUNDS, 2, half, SLOT, W), bf),
            pltpu.VMEM((ROUNDS, 2, MINE, SLOT, W), bf),
            pltpu.VMEM((DIRECT, 3, MINE, SLOT, W), bf),
            pltpu.VMEM((ROUNDS, MINE, SLOT, W), bf),
            pltpu.VMEM((tiles, SLOT * EXPERTS, LANES), f32),
            pltpu.VMEM((tiles, OWN * EXPERTS, LANES), f32),
            pltpu.VMEM((TALL, D), bf),
            pltpu.VMEM((TALL, D), bf),
            pltpu.VMEM((TALL, TALL), f32),
            pltpu.VMEM((TALL, TALL), bf),
            pltpu.VMEM((TALL, TALL), bf),
            pltpu.VMEM((TALL, D), bf),
            pltpu.VMEM((RELAYED, SIDE - 1, SLOT, W), bf),
            pltpu.VMEM((PARTS, SIDE * SLOT, PART), bf),
            dma((ROUNDS,)), dma((ROUNDS,)), dma((ROUNDS,)),
            dma((2, ROUNDS, 2)), dma((2, ROUNDS, 2)),
            dma((2, ROUNDS, 2)), dma((2, ROUNDS, 2)),
            dma((2, ROUNDS, 2)), dma((2, ROUNDS, 2)),
            dma((DIRECT, 3)), dma((DIRECT, 3)),
            dma((ROUNDS, MINE)), dma((ROUNDS,)),
            dma((RELAYED, SIDE - 1)), dma((RELAYED, SIDE - 1)),
            dma((tiles,)), dma((tiles,)), dma((tiles,)),
            dma((tiles,)), dma((tiles,)), dma((tiles,)),
            dma((PARTS, SIDE - 1)), dma((PARTS,)),
            dma((PARTS, 2 * SIDE)),
            dma((2 * CHIPS,)), dma(()),
        ],
        compiler_params=pltpu.CompilerParams(
            collective_id=0, has_side_effects=True, vmem_limit_bytes=209 * 2**18),
        name="muon",
    )(grads, mom)


def per_device(grads, momentum):
    c = lax.axis_index("dp") % 2
    mom = jnp.transpose(momentum, (1, 0, 2)).reshape(OWN * EXPERTS, D)
    mo, up = reduce_and_step(grads[0], mom)
    mo = jnp.transpose(mo.reshape(OWN, EXPERTS, D), (1, 0, 2))
    return mo, lax.dynamic_slice_in_dim(up, (OWN - 16) * c, OWN, 1)


def solution(mesh):
    return jax.shard_map(
        per_device,
        mesh=mesh,
        in_specs=(P("dp", "expert", None, None), P("expert", "dp", None)),
        out_specs=(P("expert", "dp", None), P("expert", "dp", None)),
        check_vma=False,
    )
```
